1024 devices in a mesh: grp: 16 (over x, y), ep: 64 (over z, core).
Axes of the slice: x: 4, y: 4, z: 32, core: 2. Of those that a mesh axis runs over, the one named last changes fastest.
Arguments:
- input_rows: bfloat16 [1024, 256, 2048], P(('grp', 'ep')), may hold values from -6 to 6
- cotangent_rows: bfloat16 [1024, 256, 2048], P(('grp', 'ep')), may hold values from -6 to 6
- gate_probs: float32 [1024, 256], P(('grp', 'ep')), may hold values from 0.05 to 0.5
- row_token: int32 [1024, 256], P(('grp', 'ep')), may hold values from -1 to 1023, as said below
- owner_slot: int32 [16384], P(('grp', 'ep')), may hold values from 0 to 255, as said below
- gate_proj: bfloat16 [64, 2048, 512], P('ep'), may hold values from -0.125 to 0.125
- up_proj: bfloat16 [64, 2048, 512], P('ep'), may hold values from -0.125 to 0.125
- down_proj: bfloat16 [64, 512, 2048], P('ep'), may hold values from -0.25 to 0.25
Outputs:
- input_grad: bfloat16 [16384, 2048], P(('grp', 'ep'))
- prob_grad: float32 [1024, 256], P(('grp', 'ep'))
The draws below stay inside these ranges and needn't reach their ends.
Inputs may be any that keep to these rules, and one draw needn't show every extreme that they name: `row_token`: within each expert the live rows come first, in increasing token order, then -1. Each token of a group is named by exactly 10 different experts of that group. No expert has more than 4 rows naming tokens of one ep index, and in every group one expert has exactly 4 for every ep index. `owner_slot`: value 16 * owner group + position in the owner's block; the owner lies at the same ep index. Over the tokens of one ep index it is a permutation, and every device processes exactly 1 token of each owner group.
All inputs are finite; a program needn't handle non-finite values.
Results may differ from the reference program's by a relative error of at most 0.0057.
Values may be sent and summed in bfloat16 or wider, within the bound.
A program may use at most 64 MiB of HBM per device.

```python
import math
import jax
import jax.numpy as jnp
from jax import lax

D = 2048
FF = 512
TOPK = 10
TOK_DEV = 16
EXPERTS = 64
CAP = 4
ROWS_EXP = 256
TOKENS = 16384
N_GRP = 16
N_EP = 64


def slice_members(key, popular, hot_expert):
    noise = jax.random.randint(key, (EXPERTS * CAP,), 0, 4096)
    expert_of = jnp.arange(EXPERTS * CAP, dtype=jnp.int32) // CAP
    scores = noise + popular[expert_of] * 1024 + jnp.where(expert_of == hot_expert, 65536, 0)
    scores = scores * (EXPERTS * CAP) + jnp.arange(EXPERTS * CAP, dtype=jnp.int32)
    top_values, top_index = lax.top_k(scores, TOK_DEV * TOPK)
    chosen = jnp.sort(top_index // CAP)
    picked = chosen.reshape(TOPK, TOK_DEV).T
    member = jnp.any(picked[:, :, None] == jnp.arange(EXPERTS, dtype=jnp.int32)[None, None, :], axis=1)
    return member


def group_rows(key):
    key_pop, key_hot, key_slices = jax.random.split(key, 3)
    popular = jax.random.randint(key_pop, (EXPERTS,), 0, 4)
    hot_expert = jax.random.randint(key_hot, (), 0, EXPERTS)

    def one_slice(slice_key):
        return slice_members(slice_key, popular, hot_expert)
    member = jax.vmap(one_slice)(jax.random.split(key_slices, N_EP))
    member = member.reshape(N_EP * TOK_DEV, EXPERTS).astype(jnp.int32)
    row_rank = jnp.cumsum(member, axis=0) - 1
    tokens = jnp.arange(N_EP * TOK_DEV, dtype=jnp.int32)[:, None] + jnp.zeros((1, EXPERTS), jnp.int32)
    experts = jnp.zeros((N_EP * TOK_DEV, 1), jnp.int32) + jnp.arange(EXPERTS, dtype=jnp.int32)[None, :]
    target = jnp.where(member > 0, row_rank, ROWS_EXP)
    row_table = jnp.full((EXPERTS, ROWS_EXP), -1, jnp.int32)
    return row_table.at[experts, target].set(tokens, mode='drop')


def draw_row_token(key, part):
    key = jax.random.fold_in(key, 11)
    tables = jax.vmap(group_rows)(jax.random.split(key, N_GRP))
    return tables.reshape(N_GRP * EXPERTS, ROWS_EXP)


def shuffled(key):
    return jax.random.permutation(key, TOK_DEV)


def column_owners(key):
    key_split, key_mix = jax.random.split(key)
    per_group = TOK_DEV // N_GRP
    orders = jax.vmap(shuffled)(jax.random.split(key_split, N_GRP))
    owners = jnp.arange(N_GRP, dtype=jnp.int32)[:, None] * TOK_DEV + orders
    owners = owners.reshape(N_GRP, N_GRP, per_group).transpose(1, 0, 2).reshape(N_GRP, TOK_DEV)
    mixing = jax.vmap(shuffled)(jax.random.split(key_mix, N_GRP))
    return jnp.take_along_axis(owners, mixing, axis=1)


def draw_owner_slot(key, part):
    key = jax.random.fold_in(key, 23)
    columns = jax.vmap(column_owners)(jax.random.split(key, N_EP))
    return columns.transpose(1, 0, 2).reshape(-1).astype(jnp.int32)


def level_of(rng, extent, shards, low, largest):
    factor_of, own = 1.0, jax.random.fold_in(rng, 6)
    for axis_at, shards_of in shards:
        draws = jnp.exp(jax.random.uniform(jax.random.fold_in(own, axis_at), (shards_of,), jnp.float32, low / len(shards), largest / len(shards)))
        factor_of = factor_of * jnp.repeat(draws, extent[axis_at] // shards_of).reshape([-1 if axis == axis_at else 1 for axis in range(len(extent))])
    return factor_of


def normal_values(rng, shape, width, most, cuts=(), held_as=jnp.bfloat16):
    entries = jax.random.normal(rng, shape, jnp.float32) * width
    if len(cuts) > 0:
        entries = level_of(rng, shape, cuts, -0.22, 0.18) * entries
    return jnp.clip(entries, min=-most, max=most).astype(held_as)


def setup_inputs(seed: int = 0) -> dict:
    key_of = jax.random.split(jax.random.key(seed), 9)
    return {
        "input_rows": normal_values(key_of[0], (N_GRP * EXPERTS, ROWS_EXP, D), 1.0, 6.0, ((0, 1024),)),
        "cotangent_rows": normal_values(key_of[1], (N_GRP * EXPERTS, ROWS_EXP, D), 1.0, 6.0, ((0, 1024),)),
        "gate_probs": jnp.clip(jnp.exp(math.log(0.5) - 2.3025851 * jax.random.uniform(key_of[2], (N_GRP * EXPERTS, ROWS_EXP), jnp.float32) ** level_of(key_of[2], (N_GRP * EXPERTS, ROWS_EXP), ((0, 1024),), -0.2, 0.2)), 0.05, 0.5),
        "row_token": draw_row_token(jax.random.fold_in(key_of[8], 71), 0),
        "owner_slot": draw_owner_slot(jax.random.fold_in(key_of[8], 71), 0),
        "gate_proj": normal_values(key_of[5], (EXPERTS, D, FF), D ** -0.5, 0.125, ((0, 64),)),
        "up_proj": normal_values(key_of[6], (EXPERTS, D, FF), D ** -0.5, 0.125, ((0, 64),)),
        "down_proj": normal_values(key_of[7], (EXPERTS, FF, D), FF ** -0.5, 0.25, ((0, 64),)),
    }


def expert_backward(inputs, cotangent, probs, gate_w, up_w, down_w):
    wide = jnp.float32
    best = lax.Precision.HIGHEST
    inputs = inputs.astype(wide)
    cotangent = cotangent.astype(wide)
    gate_w = gate_w.astype(wide)
    up_w = up_w.astype(wide)
    down_w = down_w.astype(wide)
    gate_pre = jnp.dot(inputs, gate_w, precision=best)
    up_pre = jnp.dot(inputs, up_w, precision=best)
    grad_act = jnp.dot(cotangent, down_w.T, precision=best)
    sigmoid_gate = jax.nn.sigmoid(gate_pre)
    activated = gate_pre * sigmoid_gate
    prob_grad = jnp.sum(grad_act * activated * up_pre, axis=1)
    scaled = probs[:, None] * grad_act
    grad_gate = (scaled * up_pre * sigmoid_gate * (1.0 + gate_pre * (1.0 - sigmoid_gate))).astype(jnp.bfloat16)
    grad_up = (scaled * activated).astype(jnp.bfloat16)
    rows_grad = jnp.dot(grad_gate.astype(wide), gate_w.T, precision=best)
    rows_grad = rows_grad + jnp.dot(grad_up.astype(wide), up_w.T, precision=best)
    return rows_grad.astype(jnp.bfloat16), prob_grad


def reference(input_rows, cotangent_rows, gate_probs, row_token, owner_slot, gate_proj, up_proj, down_proj):
    group_tokens = TOK_DEV * N_EP

    def one_group(group):
        def one_expert(expert):
            block = group * EXPERTS + expert
            return expert_backward(input_rows[block], cotangent_rows[block], gate_probs[block],
                                   gate_proj[expert], up_proj[expert], down_proj[expert])

        rows_grad, prob_grad = lax.map(one_expert, jnp.arange(EXPERTS, dtype=jnp.int32))
        tokens = lax.dynamic_slice_in_dim(row_token, (group * EXPERTS).astype(jnp.int32), EXPERTS, 0)
        prob_grad = jnp.where(tokens >= 0, prob_grad, 0.0)
        flat_tokens = jnp.where(tokens >= 0, tokens, group_tokens).reshape(-1)
        summed = jax.ops.segment_sum(rows_grad.reshape(-1, D).astype(jnp.float32), flat_tokens,
                                     num_segments=group_tokens + 1)[:group_tokens]
        return summed.astype(jnp.bfloat16), prob_grad

    token_grad, prob_grad = lax.map(one_group, jnp.arange(N_GRP, dtype=jnp.int32))
    token_grad = token_grad.reshape(N_GRP, N_EP, TOK_DEV, D)
    slots = owner_slot.reshape(N_GRP, N_EP, TOK_DEV)
    owner_group = slots // TOK_DEV
    owner_pos = slots % TOK_DEV
    column = jnp.zeros((N_GRP, N_EP, TOK_DEV), jnp.int32) + jnp.arange(N_EP, dtype=jnp.int32)[None, :, None]
    placed = jnp.zeros((N_GRP, N_EP, TOK_DEV, D), jnp.bfloat16).at[owner_group, column, owner_pos].set(token_grad)
    return placed.reshape(TOKENS, D), prob_grad.reshape(N_GRP * EXPERTS, ROWS_EXP)
```

```python
import functools

import jax
import jax.numpy as jnp
from jax import lax
from jax.experimental import pallas as pl
from jax.experimental.pallas import tpu as pltpu
from jax.sharding import PartitionSpec as P

MESH = pl.DeviceIdType.MESH
WIDE = jnp.float32
HALF = jnp.bfloat16
CHUNKS = 4
K_PARTS = 4
F_PARTS = 2


def nt(a, b):
    return lax.dot_general(a, b, (((1,), (1,)), ((), ())), preferred_element_type=WIDE)


def tn(a, b):
    return lax.dot_general(a, b, (((0,), (0,)), ((), ())), preferred_element_type=WIDE)


def nn(a, b):
    return jnp.dot(a, b, preferred_element_type=WIDE)


def iota(shape, axis):
    return lax.broadcasted_iota(jnp.int32, shape, axis)


def kernel(
    n_grp,
    n_ep,
    x_hbm,
    ct_hbm,
    probs_ref,
    tok_ref,
    own_ref,
    wg_hbm,
    wu_hbm,
    wd_hbm,
    out_ref,
    prob_ref,
    x_ref,
    ct_ref,
    wg_ref,
    wu_ref,
    wd_ref,
    gate_ref,
    up_ref,
    grad_ref,
    sorted_ref,
    rows_ref,
    give_ref,
    part_ref,
    ring_ref,
    note_send,
    note_recv,
    own_send,
    own_recv,
    wide_ref,
    back_send,
    back_recv,
    load_sem,
    note_sems,
    row_send_sem,
    row_recv_sem,
    ring_send_sem,
    ring_recv_sem,
    own_send_sem,
    own_recv_sem,
    back_send_sem,
    back_recv_sem,
):
    rows, width = x_ref.shape
    units = wg_ref.shape[1]
    tok_dev = out_ref.shape[0]
    shift = tok_dev.bit_length() - 1
    n_z = n_ep // 2
    half = n_z // 2
    side = rows // 2
    cw = width // CHUNKS
    lanes = 128
    blocks = width // lanes

    g = lax.axis_index("grp")
    e = lax.axis_index("ep")
    z = e // 2
    core = e % 2
    sibling = 2 * z + (1 - core)
    right = 2 * ((z + 1) % n_z) + core
    left = 2 * ((z + n_z - 1) % n_z) + core

    barrier = pltpu.get_barrier_semaphore()
    for peer in (sibling, right, left):
        pl.semaphore_signal(barrier, inc=1, device_id=(g, peer), device_id_type=MESH)
    for j in range(1, n_grp):
        pl.semaphore_signal(
            barrier, inc=1, device_id=((g + j) % n_grp, e), device_id_type=MESH
        )

    loads = []

    def load(src, dst):
        copy = pltpu.make_async_copy(src, dst, load_sem.at[len(loads)])
        copy.start()
        loads.append(copy)
        return copy

    load_x = load(x_hbm, x_ref)
    k_step = width // K_PARTS
    load_g = [
        load(wg_hbm.at[pl.ds(i * k_step, k_step)], wg_ref.at[pl.ds(i * k_step, k_step)])
        for i in range(K_PARTS)
    ]
    load_u = [
        load(wu_hbm.at[pl.ds(i * k_step, k_step)], wu_ref.at[pl.ds(i * k_step, k_step)])
        for i in range(K_PARTS)
    ]
    load_c = load(ct_hbm, ct_ref)
    f_step = units // F_PARTS
    load_d = [
        load(wd_hbm.at[pl.ds(i * f_step, f_step)], wd_ref.at[pl.ds(i * f_step, f_step)])
        for i in range(F_PARTS)
    ]

    tok = tok_ref[...]
    live = tok >= 0
    column = lax.shift_right_logical(jnp.where(live, tok, 0), shift)
    mine = live & ((column & 1) == core)
    other = live & ((column & 1) != core)
    line = iota((8, rows), 0)
    flags = jnp.where(
        line == 0, mine.astype(WIDE), jnp.where(line == 1, other.astype(WIDE), 0.0)
    ).astype(HALF)
    before = (iota((rows, rows), 0) < iota((rows, rows), 1)).astype(WIDE).astype(HALF)
    rank = nn(flags, before).astype(jnp.int32)
    slot = jnp.where(mine, rank[0:1], jnp.where(other, side + rank[1:2], -1))
    order = (iota((rows, rows), 0) == slot).astype(WIDE).astype(HALF)
    coded = jnp.where(
        line == 0,
        lax.shift_right_logical(column, 1).astype(WIDE),
        jnp.where(
            line == 1,
            (tok & (tok_dev - 1)).astype(WIDE),
            jnp.where(line == 2, live.astype(WIDE), 0.0),
        ),
    ).astype(HALF)
    moved = nt(coded, order)
    place = jnp.where(moved[2:3] > 0.5, moved[0:1] * tok_dev + moved[1:2], -1.0)
    place = place.astype(jnp.int32)
    note_send[...] = jnp.broadcast_to(place[:, side:], note_send.shape)
    own_send[...] = jnp.full(own_send.shape, -1, jnp.int32)
    own_send[:, 0:tok_dev] = jnp.broadcast_to(own_ref[...], (8, tok_dev))

    load_x.wait()
    for i in range(K_PARTS):
        at = pl.ds(i * k_step, k_step)
        load_g[i].wait()
        term = nn(x_ref[:, at], wg_ref[at, :])
        gate_ref[...] = term if i == 0 else gate_ref[...] + term

    pl.semaphore_wait(barrier, 3 + n_grp - 1)

    def note_copy():
        return pltpu.make_async_remote_copy(
            src_ref=note_send,
            dst_ref=note_recv,
            send_sem=note_sems.at[0],
            recv_sem=note_sems.at[1],
            device_id=(g, sibling),
            device_id_type=MESH,
        )

    def own_copy(j):
        return pltpu.make_async_remote_copy(
            src_ref=own_send,
            dst_ref=own_recv.at[pl.ds(pl.multiple_of(g * 8, 8), 8)],
            send_sem=own_send_sem.at[j],
            recv_sem=own_recv_sem.at[j],
            device_id=((g + j) % n_grp, e),
            device_id_type=MESH,
        )

    def own_copy_in(j):
        source = (g + n_grp - j) % n_grp
        return pltpu.make_async_remote_copy(
            src_ref=own_send,
            dst_ref=own_recv.at[pl.ds(pl.multiple_of(source * 8, 8), 8)],
            send_sem=own_send_sem.at[j],
            recv_sem=own_recv_sem.at[j],
            device_id=((g + j) % n_grp, e),
            device_id_type=MESH,
        )

    note_copy().start()
    for j in range(1, n_grp):
        own_copy(j).start()
    own_recv[pl.ds(pl.multiple_of(g * 8, 8), 8), :] = own_send[...]

    for i in range(K_PARTS):
        at = pl.ds(i * k_step, k_step)
        load_u[i].wait()
        term = nn(x_ref[:, at], wu_ref[at, :])
        up_ref[...] = term if i == 0 else up_ref[...] + term

    probs = jnp.transpose(jnp.broadcast_to(probs_ref[...], (lanes, rows)))[:, 0:1]
    load_c.wait()
    prob_sum = jnp.zeros((rows, lanes), WIDE)
    for i in range(F_PARTS):
        at = pl.ds(i * f_step, f_step)
        load_d[i].wait()
        grad_act = nt(ct_ref[...], wd_ref[at, :])
        gate_pre, up_pre = gate_ref[:, at], up_ref[:, at]
        sig = 1.0 / (1.0 + jnp.exp(-gate_pre))
        act = gate_pre * sig
        terms = grad_act * act * up_pre
        for j in range(f_step // lanes):
            prob_sum = prob_sum + terms[:, j * lanes : (j + 1) * lanes]
        scaled = probs * grad_act
        grad_ref[:, i * f_step : (i + 1) * f_step] = (
            scaled * up_pre * sig * (1.0 + gate_pre * (1.0 - sig))
        ).astype(HALF)
        grad_ref[:, units + i * f_step : units + (i + 1) * f_step] = (
            scaled * act
        ).astype(HALF)
    sorted_ref[...] = nn(order, grad_ref[...]).astype(HALF)

    def row_copy(c):
        return pltpu.make_async_remote_copy(
            src_ref=give_ref.at[c],
            dst_ref=rows_ref.at[c, pl.ds(side, side)],
            send_sem=row_send_sem.at[c],
            recv_sem=row_recv_sem.at[c],
            device_id=(g, sibling),
            device_id_type=MESH,
        )

    def make_rows(c):
        at = pl.ds(c * cw, cw)
        made = nt(sorted_ref[:, 0:units], wg_ref[at, :])
        made = (made + nt(sorted_ref[:, units:], wu_ref[at, :])).astype(HALF)
        give_ref[c] = made[side:]
        row_copy(c).start()
        rows_ref[c, 0:side] = made[:side]

    def ring_copy(way, c, s):
        return pltpu.make_async_remote_copy(
            src_ref=ring_ref.at[way, c, s],
            dst_ref=ring_ref.at[way, c, s + 1],
            send_sem=ring_send_sem.at[way, c, s],
            recv_sem=ring_recv_sem.at[way, c, s],
            device_id=(g, right if way == 0 else left),
            device_id_type=MESH,
        )

    def target(way, s):
        away = half - s
        return (z + away) % n_z if way == 0 else (z + n_z - away) % n_z

    def first(way, c):
        return (way + c) % 2

    def ring_start(c):
        for way in range(2):
            s = first(way, c)
            ring_ref[way, c, s] = part_ref[c, target(way, s)].astype(HALF)
            ring_copy(way, c, s).start()

    def ring_step(way, c, s):
        ring_copy(way, c, s - 1).wait_recv()
        total = ring_ref[way, c, s].astype(WIDE) + part_ref[c, target(way, s)]
        ring_ref[way, c, s] = total.astype(HALF)
        ring_copy(way, c, s).start()

    pick = None

    def make_part(c):
        row_copy(c).wait_recv()
        part_ref[c] = nn(pick, rows_ref[c]).reshape(n_z, tok_dev, cw)

    make_rows(0)
    note_copy().wait_recv()
    where_to = jnp.concatenate([place[:, :side], note_recv[0:1, :]], axis=1)
    pick = (iota((n_z * tok_dev, rows), 0) == where_to).astype(WIDE).astype(HALF)
    for c in range(1, CHUNKS):
        make_rows(c)
        make_part(c - 1)
        ring_start(c - 1)
    make_part(CHUNKS - 1)
    ring_start(CHUNKS - 1)

    prob_line = jnp.sum(jnp.transpose(prob_sum), axis=0, keepdims=True)
    prob_ref[...] = jnp.where(live, prob_line, 0.0)

    def one_step(t, carry):
        for c in range(CHUNKS):
            for way in range(2):
                ring_step(way, c, t + first(way, c))
        return carry

    lax.fori_loop(1, half - 1, one_step, 0)
    for c in range(CHUNKS):
        for way in range(2):
            if first(way, c) == 0:
                ring_step(way, c, half - 1)

    group_of = lax.shift_right_logical(own_ref[...], shift)
    to_group = (iota((n_grp, tok_dev), 0) == group_of).astype(WIDE).astype(HALF)
    for c in range(CHUNKS):
        total = part_ref[c, z]
        for way in range(2):
            ring_copy(way, c, half - 1).wait_recv()
            total = total + ring_ref[way, c, half].astype(WIDE)
        lined = nn(to_group, total.astype(HALF))
        for j in range(cw // lanes):
            wide_ref[pl.ds(c * (cw // lanes) + j, n_grp, stride=blocks), :] = lined[
                :, j * lanes : (j + 1) * lanes
            ]
    back_send[...] = wide_ref[...].astype(HALF)

    def back_copy(j, to, into):
        return pltpu.make_async_remote_copy(
            src_ref=back_send.at[pl.ds(pl.multiple_of(to * blocks, blocks), blocks)],
            dst_ref=back_recv.at[pl.ds(pl.multiple_of(into * blocks, blocks), blocks)],
            send_sem=back_send_sem.at[j],
            recv_sem=back_recv_sem.at[j],
            device_id=(to, e),
            device_id_type=MESH,
        )

    for j in range(1, n_grp):
        back_copy(j, (g + j) % n_grp, g).start()
    self_at = pl.ds(pl.multiple_of(g * blocks, blocks), blocks)
    back_recv[self_at, :] = back_send[self_at, :]

    for j in range(1, n_grp):
        own_copy_in(j).wait_recv()
    owners = own_recv[pl.ds(0, n_grp, stride=8), :]
    here = lax.shift_right_logical(owners, shift) == g
    position = jnp.sum(
        jnp.where(here, owners & (tok_dev - 1), 0), axis=1, keepdims=True
    )
    to_place = (iota((n_grp, tok_dev), 1) == position).astype(WIDE).astype(HALF)
    note_copy().wait_send()
    for c in range(CHUNKS):
        row_copy(c).wait_send()
    for j in range(1, n_grp):
        own_copy(j).wait_send()

    def drain(t, carry):
        for c in range(CHUNKS):
            for way in range(2):
                ring_copy(way, c, t + first(way, c)).wait_send()
        return carry

    lax.fori_loop(0, half - 1, drain, 0)
    for c in range(CHUNKS):
        for way in range(2):
            if first(way, c) == 0:
                ring_copy(way, c, half - 1).wait_send()

    for j in range(1, n_grp):
        back_copy(j, (g + j) % n_grp, (g + n_grp - j) % n_grp).wait_recv()
    wide_ref[...] = back_recv[...].astype(WIDE)
    for j in range(blocks):
        block = wide_ref[pl.ds(j, n_grp, stride=blocks), :].astype(HALF)
        out_ref[:, j * lanes : (j + 1) * lanes] = tn(to_place, block).astype(HALF)
    for j in range(1, n_grp):
        back_copy(j, (g + j) % n_grp, g).wait_send()


def on_device(n_grp, n_ep, x, ct, probs, tok, own, wg, wu, wd):
    rows, width = x.shape[1:]
    units = wg.shape[2]
    tok_dev = own.shape[0]
    n_z = n_ep // 2
    half = n_z // 2
    cw = width // CHUNKS
    blocks = width // 128
    anywhere = pl.BlockSpec(memory_space=pl.ANY)
    near = pl.BlockSpec(memory_space=pltpu.VMEM)
    dma = pltpu.SemaphoreType.DMA
    return pl.pallas_call(
        functools.partial(kernel, n_grp, n_ep),
        out_shape=(
            jax.ShapeDtypeStruct((tok_dev, width), HALF),
            jax.ShapeDtypeStruct((1, rows), WIDE),
        ),
        in_specs=[anywhere, anywhere, near, near, near, anywhere, anywhere, anywhere],
        out_specs=(near, near),
        scratch_shapes=[
            pltpu.VMEM((rows, width), HALF),
            pltpu.VMEM((rows, width), HALF),
            pltpu.VMEM((width, units), HALF),
            pltpu.VMEM((width, units), HALF),
            pltpu.VMEM((units, width), HALF),
            pltpu.VMEM((rows, units), WIDE),
            pltpu.VMEM((rows, units), WIDE),
            pltpu.VMEM((rows, 2 * units), HALF),
            pltpu.VMEM((rows, 2 * units), HALF),
            pltpu.VMEM((CHUNKS, rows, cw), HALF),
            pltpu.VMEM((CHUNKS, rows // 2, cw), HALF),
            pltpu.VMEM((CHUNKS, n_z, tok_dev, cw), WIDE),
            pltpu.VMEM((2, CHUNKS, half + 1, tok_dev, cw), HALF),
            pltpu.VMEM((8, rows // 2), jnp.int32),
            pltpu.VMEM((8, rows // 2), jnp.int32),
            pltpu.VMEM((8, 128), jnp.int32),
            pltpu.VMEM((8 * n_grp, 128), jnp.int32),
            pltpu.VMEM((n_grp * blocks, 128), WIDE),
            pltpu.VMEM((n_grp * blocks, 128), HALF),
            pltpu.VMEM((n_grp * blocks, 128), HALF),
            dma((2 + 2 * K_PARTS + F_PARTS,)),
            dma((2,)),
            dma((CHUNKS,)),
            dma((CHUNKS,)),
            dma((2, CHUNKS, half)),
            dma((2, CHUNKS, half)),
            dma((n_grp,)),
            dma((n_grp,)),
            dma((n_grp,)),
            dma((n_grp,)),
        ],
        compiler_params=pltpu.CompilerParams(
            collective_id=0, has_side_effects=True, vmem_limit_bytes=56 * 1024 * 1024
        ),
        cost_estimate=pl.CostEstimate(
            flops=12 * rows * width * units,
            bytes_accessed=2 * (2 * rows * width + 3 * width * units),
            transcendentals=rows * units,
        ),
        name="expert_backward",
    )(
        x.reshape(rows, width),
        ct.reshape(rows, width),
        probs,
        tok,
        own.reshape(1, tok_dev),
        wg.reshape(width, units),
        wu.reshape(width, units),
        wd.reshape(units, width),
    )


def solution(mesh):
    sizes = dict(mesh.shape)
    placed = (
        P(("grp", "ep"), None, None),
        P(("grp", "ep"), None, None),
        P(("grp", "ep"), None),
        P(("grp", "ep"), None),
        P(("grp", "ep")),
        P("ep", None, None),
        P("ep", None, None),
        P("ep", None, None),
    )
    return jax.shard_map(
        functools.partial(on_device, sizes["grp"], sizes["ep"]),
        mesh=mesh,
        in_specs=placed,
        out_specs=(P(("grp", "ep"), None), P(("grp", "ep"), None)),
        check_vma=False,
    )
```

```python
import functools

import jax
import jax.numpy as jnp
from jax import lax
from jax.experimental import pallas as pl
from jax.experimental.pallas import tpu as pltpu
from jax.sharding import PartitionSpec as P

MESH = pl.DeviceIdType.MESH
WIDE = jnp.float32
HALF = jnp.bfloat16
CHUNKS = 4
K_PARTS = 4
F_PARTS = 2


def nt(a, b):
    return lax.dot_general(a, b, (((1,), (1,)), ((), ())), preferred_element_type=WIDE)


def tn(a, b):
    return lax.dot_general(a, b, (((0,), (0,)), ((), ())), preferred_element_type=WIDE)


def nn(a, b):
    return jnp.dot(a, b, preferred_element_type=WIDE)


def iota(shape, axis):
    return lax.broadcasted_iota(jnp.int32, shape, axis)


def kernel(
    n_grp,
    n_ep,
    x_hbm,
    ct_hbm,
    probs_ref,
    tok_ref,
    own_ref,
    wg_hbm,
    wu_hbm,
    wd_hbm,
    out_ref,
    prob_ref,
    x_ref,
    ct_ref,
    wg_ref,
    wu_ref,
    wd_ref,
    gate_ref,
    up_ref,
    grad_ref,
    sorted_ref,
    made_ref,
    rows_ref,
    part_ref,
    ring_ref,
    note_send,
    note_recv,
    own_send,
    own_recv,
    wide_ref,
    back_send,
    back_recv,
    load_sem,
    note_send_sem,
    note_recv_sem,
    row_send_sem,
    row_recv_sem,
    ring_send_sem,
    ring_recv_sem,
    own_send_sem,
    own_recv_sem,
    back_send_sem,
    back_recv_sem,
):
    rows, width = x_ref.shape
    units = wg_ref.shape[1]
    tok_dev = out_ref.shape[0]
    shift = tok_dev.bit_length() - 1
    n_z = n_ep // 2
    half = n_z // 2
    steps = half // 2
    side = rows // 2
    block = side // 4
    cap = block // steps
    turns = steps // 2
    piece = block // 2
    part = 4 * piece
    cw = width // CHUNKS
    lanes = 128
    blocks = width // lanes

    g = lax.axis_index("grp")
    e = lax.axis_index("ep")
    z = e // 2
    core = e % 2

    def chip(away, flip=0):
        at = core if flip == 0 else 1 - core
        return 2 * ((z + n_z + away) % n_z) + at

    near = [chip(0, 1), chip(1), chip(1, 1), chip(-1), chip(-1, 1)]
    far = [chip(2, 1), chip(-2, 1)]
    barrier = pltpu.get_barrier_semaphore()
    for peer in near + far:
        pl.semaphore_signal(barrier, inc=1, device_id=(g, peer), device_id_type=MESH)
    for j in range(1, n_grp):
        pl.semaphore_signal(
            barrier, inc=1, device_id=((g + j) % n_grp, e), device_id_type=MESH
        )

    loads = []

    def load(src, dst):
        copy = pltpu.make_async_copy(src, dst, load_sem.at[len(loads)])
        copy.start()
        loads.append(copy)
        return copy

    load_x = load(x_hbm, x_ref)
    k_step = width // K_PARTS
    load_g = [
        load(wg_hbm.at[pl.ds(i * k_step, k_step)], wg_ref.at[pl.ds(i * k_step, k_step)])
        for i in range(K_PARTS)
    ]
    load_u = [
        load(wu_hbm.at[pl.ds(i * k_step, k_step)], wu_ref.at[pl.ds(i * k_step, k_step)])
        for i in range(K_PARTS)
    ]
    load_c = load(ct_hbm, ct_ref)
    f_step = units // F_PARTS
    load_d = [
        load(wd_hbm.at[pl.ds(i * f_step, f_step)], wd_ref.at[pl.ds(i * f_step, f_step)])
        for i in range(F_PARTS)
    ]

    tok = tok_ref[...]
    live = tok >= 0
    column = lax.shift_right_logical(jnp.where(live, tok, 0), shift)
    away = lax.shift_right_logical(column, 1) - z
    away = jnp.where(away < 0, away + n_z, away)
    odd = away & 1
    up = (away <= half) & (away > 0)
    dist = jnp.where(away <= half, away, n_z - away)
    turn = lax.shift_right_logical(half - odd - dist, 1)
    turn = jnp.where(away == 0, 0, turn)
    kind = jnp.where(up, jnp.where(odd == 1, 1, 0), jnp.where(odd == 1, 2, 3))
    flips = jnp.where(away == 0, 0, (steps - turn) & 1)
    earlier = iota((rows, rows), 0) < iota((rows, rows), 1)
    keyed = jnp.where(live, column, -1).astype(WIDE)
    down_keyed = jnp.transpose(jnp.broadcast_to(keyed, (lanes, rows)))[:, 0:1]
    rank = jnp.sum(
        jnp.where(earlier & (down_keyed == keyed), 1.0, 0.0), axis=0, keepdims=True
    ).astype(jnp.int32)
    late = jnp.where(turn >= turns, 1, 0)
    slot = late * part + kind * piece + (turn - late * turns) * cap + rank
    slot = jnp.where(((column + flips) & 1) == core, slot, slot + side)
    slot = jnp.where(live, slot, -1)
    order = (iota((rows, rows), 0) == slot).astype(WIDE).astype(HALF)
    line = iota((8, rows), 0)
    coded = jnp.where(
        line == 0,
        (tok & (tok_dev - 1)).astype(WIDE),
        jnp.where(
            line == 1,
            (live & (away > 0)).astype(WIDE),
            jnp.where(line == 2, (live & (away == 0)).astype(WIDE), 0.0),
        ),
    ).astype(HALF)
    moved = nt(coded, order)
    at_slot = iota((1, rows), 1) & (part - 1)
    kind_of = lax.shift_right_logical(at_slot, piece.bit_length() - 1)
    turn_of = lax.shift_right_logical(at_slot & (piece - 1), cap.bit_length() - 1)
    token = moved[0:1].astype(jnp.int32)
    chained = turn_of * tok_dev + token + jnp.where(kind_of >= 2, turns * tok_dev, 0)
    chained = jnp.where(moved[1:2] > 0.5, chained, -1)
    odd_kind = (kind_of == 1) | (kind_of == 2)
    kept = jnp.where(odd_kind, chained, -1)
    kept = jnp.where(moved[2:3] > 0.5, 2 * turns * tok_dev + token, kept)
    moved_on = jnp.where(odd_kind, -1, chained)
    note = jnp.where(
        iota((8, rows), 0) == 0,
        jnp.broadcast_to(kept, (8, rows)),
        jnp.broadcast_to(moved_on, (8, rows)),
    )
    note_send[0] = note[:, :side]
    note_send[1] = note[:, side:]
    own_send[...] = jnp.full(own_send.shape, -1, jnp.int32)
    own_send[:, 0:tok_dev] = jnp.broadcast_to(own_ref[...], (8, tok_dev))

    load_x.wait()
    for i in range(K_PARTS):
        at = pl.ds(i * k_step, k_step)
        load_g[i].wait()
        term = nn(x_ref[:, at], wg_ref[at, :])
        gate_ref[...] = term if i == 0 else gate_ref[...] + term
    for i in range(K_PARTS):
        at = pl.ds(i * k_step, k_step)
        load_u[i].wait()
        term = nn(x_ref[:, at], wu_ref[at, :])
        up_ref[...] = term if i == 0 else up_ref[...] + term

    pl.semaphore_wait(barrier, len(near) + len(far) + n_grp - 1)

    def note_copy(i):
        return pltpu.make_async_remote_copy(
            src_ref=note_send.at[0 if i in (1, 3) else 1],
            dst_ref=note_recv.at[i],
            send_sem=note_send_sem.at[i],
            recv_sem=note_recv_sem.at[i],
            device_id=(g, near[i]),
            device_id_type=MESH,
        )

    def own_copy(j, into):
        return pltpu.make_async_remote_copy(
            src_ref=own_send,
            dst_ref=own_recv.at[pl.ds(pl.multiple_of(into * 8, 8), 8)],
            send_sem=own_send_sem.at[j],
            recv_sem=own_recv_sem.at[j],
            device_id=((g + j) % n_grp, e),
            device_id_type=MESH,
        )

    for i in range(len(near)):
        note_copy(i).start()

    probs = jnp.transpose(jnp.broadcast_to(probs_ref[...], (lanes, rows)))[:, 0:1]
    load_c.wait()
    prob_sum = jnp.zeros((rows, lanes), WIDE)
    for i in range(F_PARTS):
        at = pl.ds(i * f_step, f_step)
        load_d[i].wait()
        grad_act = nt(ct_ref[...], wd_ref[at, :])
        gate_pre, up_pre = gate_ref[:, at], up_ref[:, at]
        sig = 1.0 / (1.0 + jnp.exp(-gate_pre))
        act = gate_pre * sig
        terms = grad_act * act * up_pre
        for j in range(f_step // lanes):
            prob_sum = prob_sum + terms[:, j * lanes : (j + 1) * lanes]
        scaled = probs * grad_act
        grad_ref[:, i * f_step : (i + 1) * f_step] = (
            scaled * up_pre * sig * (1.0 + gate_pre * (1.0 - sig))
        ).astype(HALF)
        grad_ref[:, units + i * f_step : units + (i + 1) * f_step] = (
            scaled * act
        ).astype(HALF)
    sorted_ref[...] = nn(order, grad_ref[...]).astype(HALF)

    def row_copy(c, late, i):
        if i == 0:
            count = (2 if late else 3) * piece
            src = made_ref.at[c, pl.ds(side + late * part + piece, count)]
            dst = rows_ref.at[late, c, pl.ds(part + piece, count)]
        else:
            way, flip = (i - 1) // 2, (i - 1) % 2
            at = flip * side + late * part + way * 3 * piece
            src = made_ref.at[c, pl.ds(at, piece)]
            dst = rows_ref.at[late, c, pl.ds(2 * part + (i - 1) * piece, piece)]
        return pltpu.make_async_remote_copy(
            src_ref=src,
            dst_ref=dst,
            send_sem=row_send_sem.at[c, late, i],
            recv_sem=row_recv_sem.at[c, late, i],
            device_id=(g, near[i]),
            device_id_type=MESH,
        )

    def send_rows(c, late):
        for i in (1, 2, 3, 4, 0):
            row_copy(c, late, i).start()

    nothing = jnp.zeros((piece, cw), HALF)

    def make_rows(c):
        at = pl.ds(c * cw, cw)
        made = nt(sorted_ref[:, 0:units], wg_ref[at, :])
        made = (made + nt(sorted_ref[:, units:], wu_ref[at, :])).astype(HALF)
        made_ref[c] = made
        send_rows(c, 0)
        for late in range(2):
            rows_ref[late, c, 0:part] = made[late * part : (late + 1) * part]
            rows_ref[late, c, part : part + piece] = nothing
        rows_ref[1, c, 2 * part - piece : 2 * part] = nothing

    def ring_copy(way, c, s):
        return pltpu.make_async_remote_copy(
            src_ref=ring_ref.at[way, c, s],
            dst_ref=ring_ref.at[way, c, s + 1],
            send_sem=ring_send_sem.at[way, c, s],
            recv_sem=ring_recv_sem.at[way, c, s],
            device_id=(g, near[2 + 2 * way] if s == steps - 1 else far[way]),
            device_id_type=MESH,
        )

    def own_part(way, c, s):
        late = s // turns
        at = (way * turns + s - late * turns) * tok_dev
        return part_ref[late, c, at : at + tok_dev]

    def ring_start(c):
        for way in range(2):
            ring_ref[way, c, 0] = own_part(way, c, 0).astype(HALF)
            ring_copy(way, c, 0).start()

    def ring_step(way, c, s):
        ring_copy(way, c, s - 1).wait_recv()
        total = ring_ref[way, c, s].astype(WIDE) + own_part(way, c, s)
        ring_ref[way, c, s] = total.astype(HALF)
        ring_copy(way, c, s).start()

    for c in range(CHUNKS):
        make_rows(c)
    for i in range(len(near)):
        note_copy(i).wait_recv()
    lane = iota((1, side), 1)

    def rolled(value, by):
        return pltpu.roll(value, by % side, 1) if by % side else value

    def make_pick(late):
        base = late * part
        held = jnp.where(
            lane < part,
            rolled(note_send[0, 0:1], -base),
            rolled(note_recv[0, 0:1], part - base),
        )
        passed = rolled(note_recv[4, 1:2], 3 * piece - base - 3 * piece)
        for q in (2, 1, 0):
            from_at = base + (q // 2) * 3 * piece
            passed = jnp.where(
                lane < (q + 1) * piece,
                rolled(note_recv[1 + q, 1:2], q * piece - from_at),
                passed,
            )
        to = jnp.concatenate([held, passed[:, 0:part]], axis=1)
        count = (2 * turns + 1 - late) * tok_dev
        return (iota((count, 3 * part), 0) == to).astype(WIDE).astype(HALF)

    def make_part(c, late, pick):
        for i in range(5):
            row_copy(c, late, i).wait_recv()
        made = nn(pick, rows_ref[late, c])
        part_ref[late, c, 0 : pick.shape[0]] = made

    pick = make_pick(0)
    for c in range(CHUNKS):
        make_part(c, 0, pick)
        ring_start(c)
    for c in range(CHUNKS):
        send_rows(c, 1)
    pick = make_pick(1)

    prob_line = jnp.sum(jnp.transpose(prob_sum), axis=0, keepdims=True)
    prob_ref[...] = jnp.where(live, prob_line, 0.0)

    own_recv[pl.ds(pl.multiple_of(g * 8, 8), 8), :] = own_send[...]
    to_send = list(range(1, n_grp))
    share = -(-len(to_send) // max(steps - 1, 1))
    for s in range(1, steps):
        if s == min(2, turns):
            for c in range(CHUNKS):
                make_part(c, 1, pick)
        for c in range(CHUNKS):
            for way in range(2):
                ring_step(way, c, s)
        for j in to_send[(s - 1) * share : s * share]:
            own_copy(j, g).start()

    group_of = lax.shift_right_logical(own_ref[...], shift)
    to_group = (iota((n_grp, tok_dev), 0) == group_of).astype(WIDE).astype(HALF)
    for c in range(CHUNKS):
        total = part_ref[0, c, 2 * turns * tok_dev : (2 * turns + 1) * tok_dev]
        for way in range(2):
            ring_copy(way, c, steps - 1).wait_recv()
            total = total + ring_ref[way, c, steps].astype(WIDE)
        lined = nn(to_group, total.astype(HALF))
        for j in range(cw // lanes):
            wide_ref[pl.ds(c * (cw // lanes) + j, n_grp, stride=blocks), :] = lined[
                :, j * lanes : (j + 1) * lanes
            ]
    back_send[...] = wide_ref[...].astype(HALF)

    def back_copy(j, to, into):
        return pltpu.make_async_remote_copy(
            src_ref=back_send.at[pl.ds(pl.multiple_of(to * blocks, blocks), blocks)],
            dst_ref=back_recv.at[pl.ds(pl.multiple_of(into * blocks, blocks), blocks)],
            send_sem=back_send_sem.at[j],
            recv_sem=back_recv_sem.at[j],
            device_id=(to, e),
            device_id_type=MESH,
        )

    for j in range(1, n_grp):
        back_copy(j, (g + j) % n_grp, g).start()
    self_at = pl.ds(pl.multiple_of(g * blocks, blocks), blocks)
    back_recv[self_at, :] = back_send[self_at, :]

    for j in range(1, n_grp):
        own_copy(j, (g + n_grp - j) % n_grp).wait_recv()
    owners = own_recv[pl.ds(0, n_grp, stride=8), :]
    here = lax.shift_right_logical(owners, shift) == g
    position = jnp.sum(
        jnp.where(here, owners & (tok_dev - 1), 0), axis=1, keepdims=True
    )
    to_place = (iota((n_grp, tok_dev), 1) == position).astype(WIDE).astype(HALF)
    for i in range(len(near)):
        note_copy(i).wait_send()
    for c in range(CHUNKS):
        for late in range(2):
            for i in range(5):
                row_copy(c, late, i).wait_send()
    for j in range(1, n_grp):
        own_copy(j, g).wait_send()

    for s in range(steps):
        for c in range(CHUNKS):
            for way in range(2):
                ring_copy(way, c, s).wait_send()

    for j in range(1, n_grp):
        back_copy(j, (g + j) % n_grp, (g + n_grp - j) % n_grp).wait_recv()
    wide_ref[...] = back_recv[...].astype(WIDE)
    for j in range(blocks):
        columns = wide_ref[pl.ds(j, n_grp, stride=blocks), :].astype(HALF)
        out_ref[:, j * lanes : (j + 1) * lanes] = tn(to_place, columns).astype(HALF)
    for j in range(1, n_grp):
        back_copy(j, (g + j) % n_grp, g).wait_send()


def finish(grad_ref, prob_ref, grad_out, prob_out):
    grad_out[...] = grad_ref[...]
    prob_out[...] = prob_ref[...]


def on_device(n_grp, n_ep, x, ct, probs, tok, own, wg, wu, wd):
    rows, width = x.shape[1:]
    units = wg.shape[2]
    tok_dev = own.shape[0]
    steps = n_ep // 8
    cw = width // CHUNKS
    blocks = width // 128
    anywhere = pl.BlockSpec(memory_space=pl.ANY)
    near = pl.BlockSpec(memory_space=pltpu.VMEM)
    dma = pltpu.SemaphoreType.DMA
    results = (
        jax.ShapeDtypeStruct((tok_dev, width), HALF),
        jax.ShapeDtypeStruct((1, rows), WIDE),
    )
    made = pl.pallas_call(
        functools.partial(kernel, n_grp, n_ep),
        out_shape=results,
        in_specs=[anywhere, anywhere, near, near, near, anywhere, anywhere, anywhere],
        out_specs=(near, near),
        scratch_shapes=[
            pltpu.VMEM((rows, width), HALF),
            pltpu.VMEM((rows, width), HALF),
            pltpu.VMEM((width, units), HALF),
            pltpu.VMEM((width, units), HALF),
            pltpu.VMEM((units, width), HALF),
            pltpu.VMEM((rows, units), WIDE),
            pltpu.VMEM((rows, units), WIDE),
            pltpu.VMEM((rows, 2 * units), HALF),
            pltpu.VMEM((rows, 2 * units), HALF),
            pltpu.VMEM((CHUNKS, rows, cw), HALF),
            pltpu.VMEM((2, CHUNKS, 3 * (rows // 4), cw), HALF),
            pltpu.VMEM((2, CHUNKS, (steps + 1) * tok_dev, cw), WIDE),
            pltpu.VMEM((2, CHUNKS, steps + 1, tok_dev, cw), HALF),
            pltpu.VMEM((2, 8, rows // 2), jnp.int32),
            pltpu.VMEM((5, 8, rows // 2), jnp.int32),
            pltpu.VMEM((8, 128), jnp.int32),
            pltpu.VMEM((8 * n_grp, 128), jnp.int32),
            pltpu.VMEM((n_grp * blocks, 128), WIDE),
            pltpu.VMEM((n_grp * blocks, 128), HALF),
            pltpu.VMEM((n_grp * blocks, 128), HALF),
            dma((2 + 2 * K_PARTS + F_PARTS,)),
            dma((5,)),
            dma((5,)),
            dma((CHUNKS, 2, 5)),
            dma((CHUNKS, 2, 5)),
            dma((2, CHUNKS, steps)),
            dma((2, CHUNKS, steps)),
            dma((n_grp,)),
            dma((n_grp,)),
            dma((n_grp,)),
            dma((n_grp,)),
        ],
        compiler_params=pltpu.CompilerParams(
            collective_id=0, has_side_effects=True, vmem_limit_bytes=56 * 1024 * 1024
        ),
        cost_estimate=pl.CostEstimate(
            flops=12 * rows * width * units,
            bytes_accessed=2 * (2 * rows * width + 3 * width * units),
            transcendentals=rows * units,
        ),
        name="expert_backward",
    )(
        x.reshape(rows, width),
        ct.reshape(rows, width),
        probs,
        tok,
        own.reshape(1, tok_dev),
        wg.reshape(width, units),
        wu.reshape(width, units),
        wd.reshape(units, width),
    )
    return pl.pallas_call(
        finish,
        out_shape=results,
        in_specs=[near, near],
        out_specs=(near, near),
        name="results",
    )(*made)


def solution(mesh):
    sizes = dict(mesh.shape)
    placed = (
        P(("grp", "ep"), None, None),
        P(("grp", "ep"), None, None),
        P(("grp", "ep"), None),
        P(("grp", "ep"), None),
        P(("grp", "ep")),
        P("ep", None, None),
        P("ep", None, None),
        P("ep", None, None),
    )
    return jax.shard_map(
        functools.partial(on_device, sizes["grp"], sizes["ep"]),
        mesh=mesh,
        in_specs=placed,
        out_specs=(P(("grp", "ep"), None), P(("grp", "ep"), None)),
        check_vma=False,
    )
```

```python
import functools

import jax
import jax.numpy as jnp
from jax import lax
from jax.experimental import pallas as pl
from jax.experimental.pallas import tpu as pltpu
from jax.sharding import PartitionSpec as P

MESH = pl.DeviceIdType.MESH
WIDE = jnp.float32
HALF = jnp.bfloat16
CHUNKS = 4
K_PARTS = 4
F_PARTS = 2


def nt(a, b):
    return lax.dot_general(a, b, (((1,), (1,)), ((), ())), preferred_element_type=WIDE)


def tn(a, b):
    return lax.dot_general(a, b, (((0,), (0,)), ((), ())), preferred_element_type=WIDE)


def nn(a, b):
    return jnp.dot(a, b, preferred_element_type=WIDE)


def iota(shape, axis):
    return lax.broadcasted_iota(jnp.int32, shape, axis)


def kernel(
    n_grp,
    n_ep,
    x_hbm,
    ct_hbm,
    probs_hbm,
    tok_hbm,
    own_hbm,
    wg_hbm,
    wu_hbm,
    wd_hbm,
    out_ref,
    prob_ref,
    probs_ref,
    tok_ref,
    own_ref,
    x_ref,
    ct_ref,
    wg_ref,
    wu_ref,
    wd_ref,
    gate_ref,
    up_ref,
    grad_ref,
    sorted_ref,
    made_ref,
    rows_ref,
    part_ref,
    ring_ref,
    note_send,
    note_recv,
    own_send,
    own_recv,
    wide_ref,
    back_send,
    back_recv,
    load_sem,
    note_send_sem,
    note_recv_sem,
    row_send_sem,
    row_recv_sem,
    ring_send_sem,
    ring_recv_sem,
    own_send_sem,
    own_recv_sem,
    back_send_sem,
    back_recv_sem,
):
    rows, width = x_ref.shape
    units = wg_ref.shape[1]
    tok_dev = out_ref.shape[0]
    shift = tok_dev.bit_length() - 1
    n_z = n_ep // 2
    half = n_z // 2
    steps = half // 2
    side = rows // 2
    block = side // 4
    cap = block // steps
    turns = steps // 2
    piece = block // 2
    part = 4 * piece
    cw = width // CHUNKS
    lanes = 128
    blocks = width // lanes

    g = lax.axis_index("grp")
    e = lax.axis_index("ep")
    z = e // 2
    core = e % 2

    def chip(away, flip=0):
        at = core if flip == 0 else 1 - core
        return 2 * ((z + n_z + away) % n_z) + at

    near = [chip(0, 1), chip(1), chip(1, 1), chip(-1), chip(-1, 1)]
    far = [chip(2, 1), chip(-2, 1)]
    loads = []

    def load(src, dst):
        copy = pltpu.make_async_copy(src, dst, load_sem.at[len(loads)])
        copy.start()
        loads.append(copy)
        return copy

    load_tok = load(tok_hbm, tok_ref)
    load_own = load(own_hbm, own_ref)
    load_probs = load(probs_hbm, probs_ref)
    load_x = load(x_hbm, x_ref)
    k_step = width // K_PARTS
    load_g = [
        load(wg_hbm.at[pl.ds(i * k_step, k_step)], wg_ref.at[pl.ds(i * k_step, k_step)])
        for i in range(K_PARTS)
    ]
    load_u = [
        load(wu_hbm.at[pl.ds(i * k_step, k_step)], wu_ref.at[pl.ds(i * k_step, k_step)])
        for i in range(K_PARTS)
    ]
    load_c = load(ct_hbm, ct_ref)
    f_step = units // F_PARTS
    load_d = [
        load(wd_hbm.at[pl.ds(i * f_step, f_step)], wd_ref.at[pl.ds(i * f_step, f_step)])
        for i in range(F_PARTS)
    ]

    barrier = pltpu.get_barrier_semaphore()
    for peer in near + far:
        pl.semaphore_signal(barrier, inc=1, device_id=(g, peer), device_id_type=MESH)
    for j in range(1, n_grp):
        pl.semaphore_signal(
            barrier, inc=1, device_id=((g + j) % n_grp, e), device_id_type=MESH
        )

    load_tok.wait()
    tok = tok_ref[...]
    live = tok >= 0
    column = lax.shift_right_logical(jnp.where(live, tok, 0), shift)
    away = lax.shift_right_logical(column, 1) - z
    away = jnp.where(away < 0, away + n_z, away)
    odd = away & 1
    up = (away <= half) & (away > 0)
    dist = jnp.where(away <= half, away, n_z - away)
    turn = lax.shift_right_logical(half - odd - dist, 1)
    turn = jnp.where(away == 0, 0, turn)
    kind = jnp.where(up, jnp.where(odd == 1, 1, 0), jnp.where(odd == 1, 2, 3))
    flips = jnp.where(away == 0, 0, (steps - turn) & 1)
    earlier = iota((rows, rows), 0) < iota((rows, rows), 1)
    keyed = jnp.where(live, column, -1).astype(WIDE)
    down_keyed = jnp.transpose(jnp.broadcast_to(keyed, (lanes, rows)))[:, 0:1]
    rank = jnp.sum(
        jnp.where(earlier & (down_keyed == keyed), 1.0, 0.0), axis=0, keepdims=True
    ).astype(jnp.int32)
    late = jnp.where(turn >= turns, 1, 0)
    slot = late * part + kind * piece + (turn - late * turns) * cap + rank
    slot = jnp.where(((column + flips) & 1) == core, slot, slot + side)
    slot = jnp.where(live, slot, -1)
    order = (iota((rows, rows), 0) == slot).astype(WIDE).astype(HALF)
    line = iota((8, rows), 0)
    coded = jnp.where(
        line == 0,
        (tok & (tok_dev - 1)).astype(WIDE),
        jnp.where(
            line == 1,
            (live & (away > 0)).astype(WIDE),
            jnp.where(line == 2, (live & (away == 0)).astype(WIDE), 0.0),
        ),
    ).astype(HALF)
    moved = nt(coded, order)
    at_slot = iota((1, rows), 1) & (part - 1)
    kind_of = lax.shift_right_logical(at_slot, piece.bit_length() - 1)
    turn_of = lax.shift_right_logical(at_slot & (piece - 1), cap.bit_length() - 1)
    token = moved[0:1].astype(jnp.int32)
    chained = turn_of * tok_dev + token + jnp.where(kind_of >= 2, turns * tok_dev, 0)
    chained = jnp.where(moved[1:2] > 0.5, chained, -1)
    odd_kind = (kind_of == 1) | (kind_of == 2)
    kept = jnp.where(odd_kind, chained, -1)
    kept = jnp.where(moved[2:3] > 0.5, 2 * turns * tok_dev + token, kept)
    moved_on = jnp.where(odd_kind, -1, chained)
    note = jnp.where(
        iota((8, rows), 0) == 0,
        jnp.broadcast_to(kept, (8, rows)),
        jnp.broadcast_to(moved_on, (8, rows)),
    )
    note_send[0] = note[:, :side]
    note_send[1] = note[:, side:]
    load_own.wait()
    own_send[...] = jnp.full(own_send.shape, -1, jnp.int32)
    own_send[:, 0:tok_dev] = jnp.broadcast_to(own_ref[...], (8, tok_dev))

    load_x.wait()
    for i in range(K_PARTS):
        at = pl.ds(i * k_step, k_step)
        load_g[i].wait()
        term = nn(x_ref[:, at], wg_ref[at, :])
        gate_ref[...] = term if i == 0 else gate_ref[...] + term
    for i in range(K_PARTS):
        at = pl.ds(i * k_step, k_step)
        load_u[i].wait()
        term = nn(x_ref[:, at], wu_ref[at, :])
        up_ref[...] = term if i == 0 else up_ref[...] + term

    pl.semaphore_wait(barrier, len(near) + len(far) + n_grp - 1)

    def note_copy(i):
        return pltpu.make_async_remote_copy(
            src_ref=note_send.at[0 if i in (1, 3) else 1],
            dst_ref=note_recv.at[i],
            send_sem=note_send_sem.at[i],
            recv_sem=note_recv_sem.at[i],
            device_id=(g, near[i]),
            device_id_type=MESH,
        )

    def own_copy(j, into):
        return pltpu.make_async_remote_copy(
            src_ref=own_send,
            dst_ref=own_recv.at[pl.ds(pl.multiple_of(into * 8, 8), 8)],
            send_sem=own_send_sem.at[j],
            recv_sem=own_recv_sem.at[j],
            device_id=((g + j) % n_grp, e),
            device_id_type=MESH,
        )

    for i in range(len(near)):
        note_copy(i).start()

    load_probs.wait()
    probs = jnp.transpose(jnp.broadcast_to(probs_ref[...], (lanes, rows)))[:, 0:1]
    load_c.wait()
    prob_sum = jnp.zeros((rows, lanes), WIDE)
    for i in range(F_PARTS):
        at = pl.ds(i * f_step, f_step)
        load_d[i].wait()
        grad_act = nt(ct_ref[...], wd_ref[at, :])
        gate_pre, up_pre = gate_ref[:, at], up_ref[:, at]
        sig = 1.0 / (1.0 + jnp.exp(-gate_pre))
        act = gate_pre * sig
        terms = grad_act * act * up_pre
        for j in range(f_step // lanes):
            prob_sum = prob_sum + terms[:, j * lanes : (j + 1) * lanes]
        scaled = probs * grad_act
        grad_ref[:, i * f_step : (i + 1) * f_step] = (
            scaled * up_pre * sig * (1.0 + gate_pre * (1.0 - sig))
        ).astype(HALF)
        grad_ref[:, units + i * f_step : units + (i + 1) * f_step] = (
            scaled * act
        ).astype(HALF)
    sorted_ref[...] = nn(order, grad_ref[...]).astype(HALF)

    def row_copy(c, late, i):
        if i == 0:
            count = (2 if late else 3) * piece
            src = made_ref.at[c, pl.ds(side + late * part + piece, count)]
            dst = rows_ref.at[late, c, pl.ds(part + piece, count)]
        else:
            way, flip = (i - 1) // 2, (i - 1) % 2
            at = flip * side + late * part + way * 3 * piece
            src = made_ref.at[c, pl.ds(at, piece)]
            dst = rows_ref.at[late, c, pl.ds(2 * part + (i - 1) * piece, piece)]
        return pltpu.make_async_remote_copy(
            src_ref=src,
            dst_ref=dst,
            send_sem=row_send_sem.at[c, late, i],
            recv_sem=row_recv_sem.at[c, late, i],
            device_id=(g, near[i]),
            device_id_type=MESH,
        )

    def send_rows(c, late):
        for i in (1, 2, 3, 4, 0):
            row_copy(c, late, i).start()

    nothing = jnp.zeros((piece, cw), HALF)

    def make_rows(c):
        at = pl.ds(c * cw, cw)
        made = nt(sorted_ref[:, 0:units], wg_ref[at, :])
        made = (made + nt(sorted_ref[:, units:], wu_ref[at, :])).astype(HALF)
        made_ref[c] = made
        send_rows(c, 0)
        for late in range(2):
            rows_ref[late, c, 0:part] = made[late * part : (late + 1) * part]
            rows_ref[late, c, part : part + piece] = nothing
        rows_ref[1, c, 2 * part - piece : 2 * part] = nothing

    def ring_copy(way, c, s):
        return pltpu.make_async_remote_copy(
            src_ref=ring_ref.at[way, c, s],
            dst_ref=ring_ref.at[way, c, s + 1],
            send_sem=ring_send_sem.at[way, c, s],
            recv_sem=ring_recv_sem.at[way, c, s],
            device_id=(g, near[2 + 2 * way] if s == steps - 1 else far[way]),
            device_id_type=MESH,
        )

    def own_part(way, c, s):
        late = s // turns
        at = (way * turns + s - late * turns) * tok_dev
        return part_ref[late, c, at : at + tok_dev]

    def ring_start(c):
        for way in range(2):
            ring_ref[way, c, 0] = own_part(way, c, 0).astype(HALF)
            ring_copy(way, c, 0).start()

    def ring_step(way, c, s):
        ring_copy(way, c, s - 1).wait_recv()
        total = ring_ref[way, c, s].astype(WIDE) + own_part(way, c, s)
        ring_ref[way, c, s] = total.astype(HALF)
        ring_copy(way, c, s).start()

    for c in range(CHUNKS):
        make_rows(c)
    for i in range(len(near)):
        note_copy(i).wait_recv()
    lane = iota((1, side), 1)

    def rolled(value, by):
        return pltpu.roll(value, by % side, 1) if by % side else value

    def make_pick(late):
        base = late * part
        held = jnp.where(
            lane < part,
            rolled(note_send[0, 0:1], -base),
            rolled(note_recv[0, 0:1], part - base),
        )
        passed = rolled(note_recv[4, 1:2], 3 * piece - base - 3 * piece)
        for q in (2, 1, 0):
            from_at = base + (q // 2) * 3 * piece
            passed = jnp.where(
                lane < (q + 1) * piece,
                rolled(note_recv[1 + q, 1:2], q * piece - from_at),
                passed,
            )
        to = jnp.concatenate([held, passed[:, 0:part]], axis=1)
        count = (2 * turns + 1 - late) * tok_dev
        return (iota((count, 3 * part), 0) == to).astype(WIDE).astype(HALF)

    def make_part(c, late, pick):
        for i in range(5):
            row_copy(c, late, i).wait_recv()
        made = nn(pick, rows_ref[late, c])
        part_ref[late, c, 0 : pick.shape[0]] = made

    pick = make_pick(0)
    for c in range(CHUNKS):
        make_part(c, 0, pick)
        ring_start(c)
    pick = make_pick(1)

    prob_line = jnp.sum(jnp.transpose(prob_sum), axis=0, keepdims=True)
    prob_ref[...] = jnp.where(live, prob_line, 0.0)

    own_recv[pl.ds(pl.multiple_of(g * 8, 8), 8), :] = own_send[...]
    to_send = list(range(1, n_grp))
    share = -(-len(to_send) // max(steps - 1, 1))
    for s in range(1, steps):
        if s == min(2, turns):
            for c in range(CHUNKS):
                send_rows(c, 1)
        for c in range(CHUNKS):
            if s == turns:
                make_part(c, 1, pick)
            for way in range(2):
                ring_step(way, c, s)
        for j in to_send[(s - 1) * share : s * share]:
            own_copy(j, g).start()

    group_of = lax.shift_right_logical(own_ref[...], shift)
    to_group = (iota((n_grp, tok_dev), 0) == group_of).astype(WIDE).astype(HALF)
    for c in range(CHUNKS):
        total = part_ref[0, c, 2 * turns * tok_dev : (2 * turns + 1) * tok_dev]
        for way in range(2):
            ring_copy(way, c, steps - 1).wait_recv()
            total = total + ring_ref[way, c, steps].astype(WIDE)
        lined = nn(to_group, total.astype(HALF))
        for j in range(cw // lanes):
            wide_ref[pl.ds(c * (cw // lanes) + j, n_grp, stride=blocks), :] = lined[
                :, j * lanes : (j + 1) * lanes
            ]
    back_send[...] = wide_ref[...].astype(HALF)

    def back_copy(j, to, into):
        return pltpu.make_async_remote_copy(
            src_ref=back_send.at[pl.ds(pl.multiple_of(to * blocks, blocks), blocks)],
            dst_ref=back_recv.at[pl.ds(pl.multiple_of(into * blocks, blocks), blocks)],
            send_sem=back_send_sem.at[j],
            recv_sem=back_recv_sem.at[j],
            device_id=(to, e),
            device_id_type=MESH,
        )

    for j in range(1, n_grp):
        back_copy(j, (g + j) % n_grp, g).start()
    self_at = pl.ds(pl.multiple_of(g * blocks, blocks), blocks)
    back_recv[self_at, :] = back_send[self_at, :]

    for j in range(1, n_grp):
        own_copy(j, (g + n_grp - j) % n_grp).wait_recv()
    owners = own_recv[pl.ds(0, n_grp, stride=8), :]
    here = lax.shift_right_logical(owners, shift) == g
    position = jnp.sum(
        jnp.where(here, owners & (tok_dev - 1), 0), axis=1, keepdims=True
    )
    to_place = (iota((n_grp, tok_dev), 1) == position).astype(WIDE).astype(HALF)
    for i in range(len(near)):
        note_copy(i).wait_send()
    for c in range(CHUNKS):
        for late in range(2):
            for i in range(5):
                row_copy(c, late, i).wait_send()
    for j in range(1, n_grp):
        own_copy(j, g).wait_send()

    for s in range(steps):
        for c in range(CHUNKS):
            for way in range(2):
                ring_copy(way, c, s).wait_send()

    for j in range(1, n_grp):
        back_copy(j, (g + j) % n_grp, (g + n_grp - j) % n_grp).wait_recv()
    wide_ref[...] = back_recv[...].astype(WIDE)
    for j in range(blocks):
        columns = wide_ref[pl.ds(j, n_grp, stride=blocks), :].astype(HALF)
        out_ref[:, j * lanes : (j + 1) * lanes] = tn(to_place, columns).astype(HALF)
    for j in range(1, n_grp):
        back_copy(j, (g + j) % n_grp, g).wait_send()


def finish(grad_ref, prob_ref, grad_out, prob_out):
    grad_out[...] = grad_ref[...]
    prob_out[...] = prob_ref[...]


def on_device(n_grp, n_ep, x, ct, probs, tok, own, wg, wu, wd):
    rows, width = x.shape[1:]
    units = wg.shape[2]
    tok_dev = own.shape[0]
    steps = n_ep // 8
    cw = width // CHUNKS
    blocks = width // 128
    anywhere = pl.BlockSpec(memory_space=pl.ANY)
    near = pl.BlockSpec(memory_space=pltpu.VMEM)
    dma = pltpu.SemaphoreType.DMA
    results = (
        jax.ShapeDtypeStruct((tok_dev, width), HALF),
        jax.ShapeDtypeStruct((1, rows), WIDE),
    )
    made = pl.pallas_call(
        functools.partial(kernel, n_grp, n_ep),
        out_shape=results,
        in_specs=[anywhere] * 8,
        out_specs=(near, near),
        scratch_shapes=[
            pltpu.VMEM((1, rows), WIDE),
            pltpu.VMEM((1, rows), jnp.int32),
            pltpu.VMEM((1, tok_dev), jnp.int32),
            pltpu.VMEM((rows, width), HALF),
            pltpu.VMEM((rows, width), HALF),
            pltpu.VMEM((width, units), HALF),
            pltpu.VMEM((width, units), HALF),
            pltpu.VMEM((units, width), HALF),
            pltpu.VMEM((rows, units), WIDE),
            pltpu.VMEM((rows, units), WIDE),
            pltpu.VMEM((rows, 2 * units), HALF),
            pltpu.VMEM((rows, 2 * units), HALF),
            pltpu.VMEM((CHUNKS, rows, cw), HALF),
            pltpu.VMEM((2, CHUNKS, 3 * (rows // 4), cw), HALF),
            pltpu.VMEM((2, CHUNKS, (steps + 1) * tok_dev, cw), WIDE),
            pltpu.VMEM((2, CHUNKS, steps + 1, tok_dev, cw), HALF),
            pltpu.VMEM((2, 8, rows // 2), jnp.int32),
            pltpu.VMEM((5, 8, rows // 2), jnp.int32),
            pltpu.VMEM((8, 128), jnp.int32),
            pltpu.VMEM((8 * n_grp, 128), jnp.int32),
            pltpu.VMEM((n_grp * blocks, 128), WIDE),
            pltpu.VMEM((n_grp * blocks, 128), HALF),
            pltpu.VMEM((n_grp * blocks, 128), HALF),
            dma((5 + 2 * K_PARTS + F_PARTS,)),
            dma((5,)),
            dma((5,)),
            dma((CHUNKS, 2, 5)),
            dma((CHUNKS, 2, 5)),
            dma((2, CHUNKS, steps)),
            dma((2, CHUNKS, steps)),
            dma((n_grp,)),
            dma((n_grp,)),
            dma((n_grp,)),
            dma((n_grp,)),
        ],
        compiler_params=pltpu.CompilerParams(
            collective_id=0, has_side_effects=True, vmem_limit_bytes=56 * 1024 * 1024
        ),
        cost_estimate=pl.CostEstimate(
            flops=12 * rows * width * units,
            bytes_accessed=2 * (2 * rows * width + 3 * width * units),
            transcendentals=rows * units,
        ),
        name="expert_backward",
    )(
        x.reshape(rows, width),
        ct.reshape(rows, width),
        probs,
        tok,
        own.reshape(1, tok_dev),
        wg.reshape(width, units),
        wu.reshape(width, units),
        wd.reshape(units, width),
    )
    return pl.pallas_call(
        finish,
        out_shape=results,
        in_specs=[near, near],
        out_specs=(near, near),
        name="results",
    )(*made)


def solution(mesh):
    sizes = dict(mesh.shape)
    placed = (
        P(("grp", "ep"), None, None),
        P(("grp", "ep"), None, None),
        P(("grp", "ep"), None),
        P(("grp", "ep"), None),
        P(("grp", "ep")),
        P("ep", None, None),
        P("ep", None, None),
        P("ep", None, None),
    )
    return jax.shard_map(
        functools.partial(on_device, sizes["grp"], sizes["ep"]),
        mesh=mesh,
        in_specs=placed,
        out_specs=(P(("grp", "ep"), None), P(("grp", "ep"), None)),
        check_vma=False,
    )
```
